32 devices in a mesh: gx: 2 (over core), gy: 4 (over y, x), gz: 4 (over z).
Axes of the slice: x: 2, y: 2, z: 4, core: 2. Of those that a mesh axis runs over, the one named last changes fastest.
Arguments:
- dual_matrix: float32 [2, 4, 4, 1536, 1536], P('gx', 'gy', 'gz'), may hold values from -1 to 4, as said below
- modes: float32 [2, 4, 4, 6, 1536], P('gx', 'gy', 'gz'), may hold values from -0.15625 to 0.15625
- coarse_rows: float32 [192, 192], P(('gx', 'gy', 'gz')), may hold values from -0.2 to 0.4, as said below
- loads: float32 [2, 4, 4, 8, 6, 128], P('gx', 'gy', 'gz'), may hold values from -40 to 40
- face_counts: int32 [2, 4, 4, 3], replicated, may hold values from 32 to 128
- contact: int32 [2, 4, 4, 6, 128], P('gx', 'gy', 'gz'), may hold values 0 or 1
Outputs:
- multipliers: float32 [2, 4, 4, 8, 6, 128], P('gx', 'gy', 'gz')
- residual: float32 [2, 4, 4, 8, 6, 128], P('gx', 'gy', 'gz')
The draws below stay inside these ranges and needn't reach their ends.
Inputs may be any that keep to these rules, and one draw needn't show every extreme that they name: `dual_matrix`: every subdomain's matrix is symmetric positive definite. `coarse_rows`: the coarse operator is symmetric positive definite.
All inputs are finite; a program needn't handle non-finite values. No bound on the sum of `contact` on one device may be relied on, other than what follows from the above.
Results may differ from the reference program's by a relative error of at most 0.0003.
Values sent between devices are 32-bit elements; how exact they have to be, the bound alone decides.
A program may use at most 128 MiB of HBM per device.

```python
import math
import jax
import jax.numpy as jnp
from jax import lax

FH = 128
LOCAL = 1536
RIGID = 6
CASES = 8
ITERS = 4
MODES = 192
N_GX = 2
N_GY = 4
N_GZ = 4


def symmetric_part(key, shape, width):
    raw = jax.random.normal(key, shape, jnp.float32)
    return (raw + jnp.swapaxes(raw, -1, -2)) * (1.0 / math.sqrt(2.0 * width))


def draw_dual_matrix(key, part):
    first, second = jax.random.split(jax.random.fold_in(key, 23))
    shape = (N_GX, N_GY, N_GZ, LOCAL, LOCAL)
    off_part = 0.4 * symmetric_part(first, shape, LOCAL)
    diagonal = jnp.exp(jax.random.uniform(second, shape[:-1], jnp.float32, 0.0, math.log(4.0)))
    identity = jnp.eye(LOCAL, dtype=jnp.float32)
    return (off_part * (1.0 - identity) + identity * diagonal[..., None]).astype(jnp.float32)


def draw_coarse_rows(key, part):
    first = jax.random.fold_in(key, 31)
    off_part = 0.3 * symmetric_part(first, (MODES, MODES), MODES)
    identity = jnp.eye(MODES, dtype=jnp.float32)
    return (0.4 * (identity + off_part * (1.0 - identity))).astype(jnp.float32)


def draw_loads(key, part):
    first = jax.random.fold_in(jax.random.fold_in(key, 11), 0)
    shape = (N_GX, N_GY, N_GZ, CASES, 6, FH)
    rising = 1.0 + 2.0 * jnp.arange(N_GX, dtype=jnp.float32) / max(N_GX - 1, 1)
    rising = rising.reshape(N_GX, 1, 1, 1, 1, 1)
    values = jax.random.normal(first, shape, jnp.float32)
    return (values * rising).astype(jnp.float32)


def touch_ends(values, own_key, smallest, largest):
    dims = values.shape
    place = [jax.random.randint(jax.random.fold_in(own_key, axis), (), 0, dims[axis]) for axis in range(len(dims))]
    values = values.at[tuple(place)].set(smallest)
    longest = dims.index(max(dims))
    place[longest] = (place[longest] + 1) % dims[longest]
    return values.at[tuple(place)].set(largest)


def levels(key, shape, shards, least, high):
    def one(dim, parts):
        draws = jax.random.uniform(jax.random.fold_in(jax.random.fold_in(key, 6), dim), (parts,), jnp.float32, least / len(shards), high / len(shards))
        return jnp.repeat(jnp.exp(draws), shape[dim] // parts).reshape((-1,) + (1,) * (len(shape) - dim - 1))

    gain = one(*shards[0])
    for cut in shards[1:]:
        gain = gain * one(*cut)
    return gain


def noise(key, extent, deviation, limit, cuts=(), kind=jnp.bfloat16):
    result = deviation * jax.random.normal(key, extent, jnp.float32)
    if cuts:
        result = result * levels(key, extent, cuts, -0.22, 0.18)
    return jnp.clip(result, -limit, limit).astype(kind)


def setup_inputs(seed: int = 0) -> dict:
    key_of = jax.random.split(jax.random.key(seed), 7)
    return {
        "dual_matrix": draw_dual_matrix(jax.random.fold_in(key_of[6], 71), 0),
        "modes": noise(key_of[1], (N_GX, N_GY, N_GZ, RIGID, LOCAL), LOCAL ** -0.5, 0.15625, ((0, 2), (1, 4), (2, 4)), jnp.float32),
        "coarse_rows": draw_coarse_rows(jax.random.fold_in(key_of[6], 71), 0),
        "loads": draw_loads(jax.random.fold_in(key_of[6], 71), 0),
        "face_counts": touch_ends(jax.random.randint(key_of[4], (N_GX, N_GY, N_GZ, 3), FH // 4, FH + 1), jax.random.fold_in(key_of[4], 1), FH // 4, FH).astype(jnp.int32),
        "contact": touch_ends((jax.random.randint(key_of[5], (N_GX, N_GY, N_GZ, 6, FH), 0, 3) < 1).astype(jnp.int32), jax.random.fold_in(key_of[5], 1), 0, 1),
    }


highest = lax.Precision.HIGHEST


def spread_faces(owned_vec):
    faces = []
    for grid_axis in range(3):
        below = jnp.roll(owned_vec, 1, axis=grid_axis)
        above = jnp.roll(owned_vec, -1, axis=grid_axis)
        faces.append(jnp.concatenate([below[..., 2 * grid_axis + 1, :], owned_vec[..., 2 * grid_axis, :]], axis=-1))
        faces.append(jnp.concatenate([owned_vec[..., 2 * grid_axis + 1, :], above[..., 2 * grid_axis, :]], axis=-1))
    return jnp.stack(faces, axis=-2)


def collect_faces(local_form):
    half_width = local_form.shape[-1] // 2
    pieces = []
    for grid_axis in range(3):
        below = jnp.roll(local_form, 1, axis=grid_axis)
        above = jnp.roll(local_form, -1, axis=grid_axis)
        pieces.append(local_form[..., 2 * grid_axis, half_width:] + below[..., 2 * grid_axis + 1, half_width:])
        pieces.append(local_form[..., 2 * grid_axis + 1, :half_width] + above[..., 2 * grid_axis, :half_width])
    return jnp.stack(pieces, axis=-2)


def apply_dual(vector, dual_matrix, active):
    local_form = spread_faces(vector)
    flattened = local_form.reshape(local_form.shape[:4] + (-1,))
    dual_image = jnp.einsum('abcnm,abckm->abckn', dual_matrix, flattened, precision=highest)
    return collect_faces(dual_image.reshape(local_form.shape)) * active


def project(vector, modes, coarse_rows, active):
    local_form = spread_faces(vector)
    flattened = local_form.reshape(local_form.shape[:4] + (-1,))
    on_modes = jnp.einsum('abcjm,abckm->abcjk', modes, flattened, precision=highest)
    stacked = on_modes.reshape(-1, on_modes.shape[-1])
    weights = jnp.dot(coarse_rows, stacked, precision=highest).reshape(on_modes.shape)
    correction = jnp.einsum('abcjk,abcjm->abckm', weights, modes, precision=highest)
    return vector - collect_faces(correction.reshape(local_form.shape)) * active


def inner(first, second):
    return jnp.sum(first * second, axis=(0, 1, 2, 4, 5))[:, None, None]


def reference(dual_matrix, modes, coarse_rows, loads, face_counts, contact):
    positions = jnp.arange(loads.shape[-1], dtype=jnp.int32)
    masks = []
    for grid_axis in range(3):
        lower_count = jnp.roll(face_counts, 1, axis=grid_axis)[..., grid_axis]
        masks.append((positions < lower_count[..., None]).astype(jnp.float32))
        masks.append((positions < face_counts[..., grid_axis][..., None]).astype(jnp.float32))
    active = jnp.stack(masks, axis=-2)[:, :, :, None]
    is_contact = contact[:, :, :, None] == 1
    residual = loads * active
    multipliers = jnp.zeros_like(residual)
    precond = project(residual, modes, coarse_rows, active)
    direction = precond
    energy = inner(residual, precond)
    for rounds in range(ITERS):
        dual_image = apply_dual(direction, dual_matrix, active)
        step_size = energy / inner(direction, dual_image)
        multipliers = multipliers + step_size * direction
        multipliers = jnp.where(is_contact, jnp.maximum(multipliers, 0.0), multipliers)
        residual = residual - step_size * dual_image
        if rounds + 1 < ITERS:
            precond = project(residual, modes, coarse_rows, active)
            energy_next = inner(residual, precond)
            direction = precond + (energy_next / energy) * direction
            energy = energy_next
    return multipliers, residual
```

```python
import functools
import math

import jax
import jax.numpy as jnp
from jax import lax
from jax.experimental import pallas as pl
from jax.experimental.pallas import tpu as pltpu
from jax.sharding import PartitionSpec as P

ITERS = 4
NAMES = ("gx", "gy", "gz")
highest = lax.Precision.HIGHEST
SCALARS = 56


def dot_nt(a, b):
    return lax.dot_general(
        a, b, (((1,), (1,)), ((), ())), precision=highest, preferred_element_type=jnp.float32
    )


def dot_nn(a, b):
    return lax.dot_general(
        a, b, (((1,), (0,)), ((), ())), precision=highest, preferred_element_type=jnp.float32
    )


def kernel(
    sizes,
    k_hbm,
    modes,
    crows,
    loads,
    counts,
    contact,
    lam_out,
    res_out,
    kbuf,
    khi,
    klo,
    bmat,
    c7,
    act,
    rvec,
    yvec,
    faces_in,
    gath,
    k_sem,
    set_send,
    set_recv,
    face_send,
    face_recv,
    gath_send,
    gath_recv,
):
    cases = loads.shape[0]
    half = loads.shape[2]
    full = 2 * half
    local = bmat.shape[1]
    rigid = modes.shape[0]
    n = math.prod(sizes)
    pos = [lax.axis_index(name) for name in NAMES]
    me = (pos[0] * sizes[1] + pos[1]) * sizes[2] + pos[2]

    def neighbour(f):
        a = f // 2
        step = 1 if f % 2 else sizes[a] - 1
        where = list(pos)
        where[a] = lax.rem(pos[a] + step, sizes[a])
        return tuple(where)

    nbrs = [neighbour(f) for f in range(6)]

    def own_tile(f):
        return 2 * f + (1 - f % 2)

    def tile(f_tile):
        return slice(f_tile * half, (f_tile + 1) * half)

    def k_copy(c):
        return pltpu.make_async_copy(
            k_hbm.at[:, pl.ds(c * full, full)], kbuf.at[c], k_sem.at[c]
        )

    for c in range(6):
        k_copy(c).start()

    bmat[...] = jnp.zeros_like(bmat)
    c7[...] = jnp.zeros_like(c7)
    bmat[0:rigid, :] = modes[...]
    c7[0:rigid, 0 : crows.shape[1]] = crows[...]

    lane = lax.broadcasted_iota(jnp.int32, (cases, half), 1)
    for f in range(6):
        a = f // 2
        where = list(pos) if f % 2 else list(nbrs[f])
        count = counts[where[0], where[1], where[2], a]
        mask = (lane < count).astype(jnp.float32)
        act[:, tile(2 * f)] = mask
        act[:, tile(2 * f + 1)] = mask
        rvec[:, tile(own_tile(f))] = loads[:, f, :] * mask

    barrier = pltpu.get_barrier_semaphore()

    def greet(k, carry):
        pl.semaphore_signal(
            barrier,
            inc=1,
            device_id=lax.rem(me + k, n),
            device_id_type=pl.DeviceIdType.LOGICAL,
        )
        return carry

    lax.fori_loop(1, n, greet, 0)
    pl.semaphore_wait(barrier, n - 1)

    def remote(src, dst, send, recv, f):
        return pltpu.make_async_remote_copy(
            src_ref=src,
            dst_ref=dst,
            send_sem=send,
            recv_sem=recv,
            device_id=nbrs[f],
            device_id_type=pl.DeviceIdType.MESH,
        )

    def set_copies(f):
        opp = f ^ 1
        h = 1 - f % 2
        rows = pl.ds(8 * (opp + 1), 8)
        return [
            remote(
                rvec.at[:, pl.ds((2 * f + h) * half, half)],
                rvec.at[:, pl.ds((2 * opp + h) * half, half)],
                set_send.at[f, 0],
                set_recv.at[opp, 0],
                f,
            ),
            remote(
                bmat.at[pl.ds(0, 8), pl.ds(f * full, full)],
                bmat.at[rows, pl.ds(opp * full, full)],
                set_send.at[f, 1],
                set_recv.at[opp, 1],
                f,
            ),
            remote(c7.at[pl.ds(0, 8)], c7.at[rows], set_send.at[f, 2], set_recv.at[opp, 2], f),
        ]

    set_all = [set_copies(f) for f in range(6)]
    for i in range(3):
        for f in range(6):
            set_all[f][i].start()

    def split_chunk(c):
        k_copy(c).wait()
        step = 256

        def body(i, carry):
            rows = pl.ds(pl.multiple_of(i * step, step), step)
            x = kbuf[c, rows, :]
            hi = x.astype(jnp.bfloat16)
            khi[c, rows, :] = hi
            klo[c, rows, :] = (x - hi.astype(jnp.float32)).astype(jnp.bfloat16)
            return carry

        lax.fori_loop(0, local // step, body, 0)

    def send_message(p, message):
        rolled = pltpu.roll(message, half // 2, 1)
        packed = jnp.where(
            lane[0 : cases // 2] < half // 2, message[0 : cases // 2], rolled[cases // 2 :]
        )
        gath[p, me] = packed

        def body(k, carry):
            pltpu.make_async_remote_copy(
                src_ref=gath.at[p, me],
                dst_ref=gath.at[p, me],
                send_sem=gath_send.at[p],
                recv_sem=gath_recv.at[p],
                device_id=lax.rem(me + k, n),
                device_id_type=pl.DeviceIdType.LOGICAL,
            ).start()
            return carry

        lax.fori_loop(1, n, body, 0)

    def gather_bytes(p):
        block = gath.at[p, pl.ds(0, n - 1)]
        return pltpu.make_async_remote_copy(
            src_ref=block,
            dst_ref=block,
            send_sem=gath_send.at[p],
            recv_sem=gath_recv.at[p],
            device_id=lax.rem(me + 1, n),
            device_id_type=pl.DeviceIdType.LOGICAL,
        )

    def received(p):
        packed = gath[p]
        other = pltpu.roll(packed.reshape(n * cases // 2, half), half // 2, 1).reshape(
            packed.shape
        )
        return jnp.concatenate([packed, other], axis=1)

    tiles_e = c7.shape[1] // half

    def coarse_sum(blocks, only_own):
        terms = blocks
        if not only_own:
            flat = blocks.reshape(n * cases, half)
            for f in range(6):
                moved = pltpu.roll(flat, half - 8 * (f + 1), 1).reshape(
                    sizes + (cases, half)
                )
                moved = jnp.roll(moved, 1 if f % 2 else -1, axis=f // 2)
                terms = terms + moved.reshape(n, cases, half)
        sums = [jnp.zeros((cases, half), jnp.float32) for _ in range(tiles_e)]
        for s in range(n):
            low = rigid * s
            moved = pltpu.roll(terms[s], low % half, 1) if low % half else terms[s]
            for q in range(low // half, (low + rigid - 1) // half + 1):
                at = lane + half * q
                sums[q] = jnp.where((at >= low) & (at < low + rigid), moved, sums[q])
        return jnp.concatenate(sums, axis=1)

    def own_inner(first, second):
        total = jnp.zeros((cases, half), jnp.float32)
        for f in range(6):
            cut = tile(own_tile(f))
            total = total + first[:, cut] * second[:, cut]
        return jnp.sum(total, axis=1, keepdims=True)

    def all_inner(first, second):
        total = jnp.zeros((cases, half), jnp.float32)
        for t in range(12):
            total = total + first[:, tile(t)] * second[:, tile(t)]
        return jnp.sum(total, axis=1, keepdims=True)

    split_chunk(0)
    split_chunk(1)
    for f in range(6):
        for i in range(2):
            set_all[f][i].wait_recv()
    residual = rvec[...]
    first_terms = dot_nt(residual, bmat[0:8, :])
    send_message(
        0, jnp.concatenate([first_terms, jnp.zeros((cases, half - 8), jnp.float32)], axis=1)
    )
    for c in range(2, 6):
        split_chunk(c)
    for f in range(6):
        set_all[f][2].wait_recv()
        for i in range(3):
            set_all[f][i].wait_send()
    gather_bytes(0).wait_recv()
    alpha = dot_nt(coarse_sum(received(0), True), c7[...])
    active = act[...]
    z = residual - active * dot_nn(alpha, bmat[...])

    face_copies = []
    lam = [jnp.zeros((cases, half), jnp.float32) for _ in range(6)]
    direction = image = alpha_image = energy = curvature = None
    for it in range(ITERS):
        last = it + 1 == ITERS
        p = it + 1
        hi = z.astype(jnp.bfloat16)
        lo = (z - hi.astype(jnp.float32)).astype(jnp.bfloat16)
        parts = jnp.concatenate([hi, lo], axis=0)
        copies = []
        ys = []
        for f in range(6):
            yf = jnp.dot(parts, khi[f], preferred_element_type=jnp.float32) + jnp.dot(
                parts, klo[f], preferred_element_type=jnp.float32
            )
            yf = yf[0:cases] + yf[cases:]
            yvec[it, f] = yf
            copy = remote(
                yvec.at[it, f], faces_in.at[it, f ^ 1], face_send.at[it, f],
                face_recv.at[it, f ^ 1], f,
            )
            copy.start()
            copies.append(copy)
            ys.append(yf)
        y = jnp.concatenate(ys, axis=1)
        scalars = [all_inner(z, y), own_inner(rvec, z)]
        if it:
            scalars.append(own_inner(z, image))
        if last:
            message = jnp.zeros((cases, half), jnp.float32)
        else:
            terms = dot_nt(y * active, bmat[...])
            message = jnp.concatenate([terms, jnp.zeros_like(terms)], axis=1)
        for i, value in enumerate(scalars):
            message = jnp.where(lane == SCALARS + i, value, message)
        send_message(p, message)

        for f in range(6):
            copies[f].wait_recv()
        y = jnp.concatenate([ys[f] + faces_in[it, f] for f in range(6)], axis=1) * active
        gather_bytes(p).wait_recv()
        blocks = received(p)
        totals = jnp.sum(blocks, axis=0)
        along = totals[:, SCALARS : SCALARS + 1]
        energy_next = totals[:, SCALARS + 1 : SCALARS + 2]
        if it == 0:
            direction, image, curvature = z, y, along
        else:
            ratio = energy_next / energy
            across = totals[:, SCALARS + 2 : SCALARS + 3]
            direction = z + ratio * direction
            image = y + ratio * image
            curvature = along + 2.0 * ratio * across + ratio * ratio * curvature
        energy = energy_next
        step_size = energy / curvature
        rvec[...] = rvec[...] - step_size * image
        if not last:
            alpha_y = dot_nt(coarse_sum(blocks, False), c7[...])
            alpha_image = alpha_y if it == 0 else alpha_y + ratio * alpha_image
            alpha = alpha - step_size * alpha_image
            z = rvec[...] - active * dot_nn(alpha, bmat[...])
        for f in range(6):
            updated = lam[f] + step_size * direction[:, tile(own_tile(f))]
            lam[f] = jnp.where(contact[f : f + 1, :] == 1, jnp.maximum(updated, 0.0), updated)
        face_copies.extend(copies)

    for f in range(6):
        lam_out[:, f, :] = lam[f]
        res_out[:, f, :] = rvec[:, tile(own_tile(f))]
    for copy in face_copies:
        copy.wait_send()
    for p in range(ITERS + 1):
        gather_bytes(p).wait_send()


def on_device(sizes, dual_matrix, modes, coarse_rows, loads, face_counts, contact):
    cases, faces, half = loads.shape[3:]
    local = dual_matrix.shape[-1]
    rigid = modes.shape[-2]
    full = 2 * half
    n = math.prod(sizes)
    width = -(-coarse_rows.shape[1] // half) * half
    vmem = pl.BlockSpec(memory_space=pltpu.VMEM)
    dma = pltpu.SemaphoreType.DMA
    f32 = jnp.float32
    out = jax.ShapeDtypeStruct((cases, faces, half), f32)
    lam, res = pl.pallas_call(
        functools.partial(kernel, sizes),
        out_shape=(out, out),
        in_specs=[
            pl.BlockSpec(memory_space=pl.ANY),
            vmem,
            vmem,
            vmem,
            pl.BlockSpec(memory_space=pltpu.SMEM),
            vmem,
        ],
        out_specs=(vmem, vmem),
        scratch_shapes=[
            pltpu.VMEM((faces, local, full), f32),
            pltpu.VMEM((faces, local, full), jnp.bfloat16),
            pltpu.VMEM((faces, local, full), jnp.bfloat16),
            pltpu.VMEM((64, local), f32),
            pltpu.VMEM((64, width), f32),
            pltpu.VMEM((cases, local), f32),
            pltpu.VMEM((cases, local), f32),
            pltpu.VMEM((ITERS, faces, cases, full), f32),
            pltpu.VMEM((ITERS, faces, cases, full), f32),
            pltpu.VMEM((ITERS + 1, n, cases // 2, half), f32),
            dma((faces,)),
            dma((faces, 3)),
            dma((faces, 3)),
            dma((ITERS, faces)),
            dma((ITERS, faces)),
            dma((ITERS + 1,)),
            dma((ITERS + 1,)),
        ],
        compiler_params=pltpu.CompilerParams(
            collective_id=0, has_side_effects=True, vmem_limit_bytes=48 * 1024 * 1024
        ),
    )(
        dual_matrix.reshape(local, local),
        modes.reshape(rigid, local),
        coarse_rows,
        loads.reshape(cases, faces, half),
        face_counts,
        contact.reshape(faces, half),
    )
    return lam.reshape(loads.shape), res.reshape(loads.shape)


def solution(mesh):
    sizes = tuple(mesh.shape[name] for name in NAMES)
    return jax.shard_map(
        functools.partial(on_device, sizes),
        mesh=mesh,
        in_specs=(
            P("gx", "gy", "gz", None, None),
            P("gx", "gy", "gz", None, None),
            P(("gx", "gy", "gz"), None),
            P("gx", "gy", "gz", None, None, None),
            P(),
            P("gx", "gy", "gz", None, None),
        ),
        out_specs=(P("gx", "gy", "gz", None, None, None), P("gx", "gy", "gz", None, None, None)),
        check_vma=False,
    )
```

```python
import functools
import math

import jax
import jax.numpy as jnp
from jax import lax
from jax.experimental import pallas as pl
from jax.experimental.pallas import tpu as pltpu
from jax.sharding import PartitionSpec as P

ITERS = 4
NAMES = ("gx", "gy", "gz")
SCALARS = 56


def split(x):
    hi = x.astype(jnp.bfloat16)
    return hi, (x - hi.astype(jnp.float32)).astype(jnp.bfloat16)


def split_dot(parts, hi, lo, contract):
    dims = (((1,), (contract,)), ((), ()))
    both = lax.dot_general(parts, hi, dims, preferred_element_type=jnp.float32)
    both = both + lax.dot_general(parts, lo, dims, preferred_element_type=jnp.float32)
    rows = parts.shape[0] // 2
    return both[0:rows] + both[rows:]


def dot_nt(a, hi, lo):
    return split_dot(jnp.concatenate(split(a), axis=0), hi, lo, 1)


def dot_nn(a, hi, lo):
    return split_dot(jnp.concatenate(split(a), axis=0), hi, lo, 0)


def kernel(
    sizes,
    k_hbm,
    modes_in,
    crows_in,
    loads_in,
    counts,
    contact_in,
    lam_out,
    res_out,
    kbuf,
    khi,
    klo,
    bmat,
    c7,
    act,
    rvec,
    yvec,
    faces_in,
    gath,
    modes,
    crows,
    loads,
    contact,
    bhi,
    blo,
    chi,
    clo,
    k_sem,
    in_sem,
    set_send,
    set_recv,
    face_send,
    face_recv,
    gath_send,
    gath_recv,
):
    cases = loads.shape[1]
    half = loads.shape[2]
    full = 2 * half
    local = bmat.shape[1]
    rigid = modes_in.shape[0]
    n = math.prod(sizes)
    pos = [lax.axis_index(name) for name in NAMES]
    me = (pos[0] * sizes[1] + pos[1]) * sizes[2] + pos[2]

    def neighbour(f):
        a = f // 2
        step = 1 if f % 2 else sizes[a] - 1
        where = list(pos)
        where[a] = lax.rem(pos[a] + step, sizes[a])
        return tuple(where)

    nbrs = [neighbour(f) for f in range(6)]

    def own_tile(f):
        return 2 * f + (1 - f % 2)

    def tile(f_tile):
        return slice(f_tile * half, (f_tile + 1) * half)

    def k_copy(c):
        return pltpu.make_async_copy(
            k_hbm.at[:, pl.ds(c * full, full)], kbuf.at[c], k_sem.at[c]
        )

    small = [
        pltpu.make_async_copy(src, dst, in_sem.at[i])
        for i, (src, dst) in enumerate(
            ((loads_in, loads), (modes_in, modes), (crows_in, crows), (contact_in, contact))
        )
    ]
    for copy in small:
        copy.start()
    for c in range(6):
        k_copy(c).start()

    bmat[...] = jnp.zeros_like(bmat)
    c7[...] = jnp.zeros_like(c7)
    barrier = pltpu.get_barrier_semaphore()

    def greet(k, carry):
        pl.semaphore_signal(
            barrier,
            inc=1,
            device_id=lax.rem(me + k, n),
            device_id_type=pl.DeviceIdType.LOGICAL,
        )
        return carry

    lax.fori_loop(1, n, greet, 0)
    for copy in small:
        copy.wait()
    for m in range(rigid):
        bmat[m : m + 1, :] = modes[m]
    c7[0:rigid, 0 : crows.shape[1]] = crows[...]

    lane = lax.broadcasted_iota(jnp.int32, (cases, half), 1)
    for f in range(6):
        a = f // 2
        where = list(pos) if f % 2 else list(nbrs[f])
        count = counts[where[0], a, where[1], where[2]]
        mask = (lane < count).astype(jnp.float32)
        act[:, tile(2 * f)] = mask
        act[:, tile(2 * f + 1)] = mask
        rvec[:, tile(own_tile(f))] = loads[f] * mask

    pl.semaphore_wait(barrier, n - 1)

    def remote(src, dst, send, recv, f):
        return pltpu.make_async_remote_copy(
            src_ref=src,
            dst_ref=dst,
            send_sem=send,
            recv_sem=recv,
            device_id=nbrs[f],
            device_id_type=pl.DeviceIdType.MESH,
        )

    def set_copies(f):
        opp = f ^ 1
        h = 1 - f % 2
        rows = pl.ds(8 * (opp + 1), 8)
        return [
            remote(
                rvec.at[:, pl.ds((2 * f + h) * half, half)],
                rvec.at[:, pl.ds((2 * opp + h) * half, half)],
                set_send.at[f, 0],
                set_recv.at[opp, 0],
                f,
            ),
            remote(
                bmat.at[pl.ds(0, 8), pl.ds(f * full, full)],
                bmat.at[rows, pl.ds(opp * full, full)],
                set_send.at[f, 1],
                set_recv.at[opp, 1],
                f,
            ),
            remote(c7.at[pl.ds(0, 8)], c7.at[rows], set_send.at[f, 2], set_recv.at[opp, 2], f),
        ]

    set_all = [set_copies(f) for f in range(6)]
    for i in range(3):
        for f in range(6):
            set_all[f][i].start()

    def split_chunk(c):
        k_copy(c).wait()
        step = 256

        def body(i, carry):
            rows = pl.ds(pl.multiple_of(i * step, step), step)
            x = kbuf[c, rows, :]
            khi[c, rows, :], klo[c, rows, :] = split(x)
            return carry

        lax.fori_loop(0, local // step, body, 0)

    def send_message(p, message):
        rolled = pltpu.roll(message, half // 2, 1)
        packed = jnp.where(
            lane[0 : cases // 2] < half // 2, message[0 : cases // 2], rolled[cases // 2 :]
        )
        gath[p, me] = packed

        def body(k, carry):
            pltpu.make_async_remote_copy(
                src_ref=gath.at[p, me],
                dst_ref=gath.at[p, me],
                send_sem=gath_send.at[p],
                recv_sem=gath_recv.at[p],
                device_id=lax.rem(me + k, n),
                device_id_type=pl.DeviceIdType.LOGICAL,
            ).start()
            return carry

        lax.fori_loop(1, n, body, 0)

    def gather_bytes(p):
        block = gath.at[p, pl.ds(0, n - 1)]
        return pltpu.make_async_remote_copy(
            src_ref=block,
            dst_ref=block,
            send_sem=gath_send.at[p],
            recv_sem=gath_recv.at[p],
            device_id=lax.rem(me + 1, n),
            device_id_type=pl.DeviceIdType.LOGICAL,
        )

    def received(p):
        packed = gath[p]
        other = pltpu.roll(packed.reshape(n * cases // 2, half), half // 2, 1).reshape(
            packed.shape
        )
        return jnp.concatenate([packed, other], axis=1)

    tiles_e = c7.shape[1] // half

    def coarse_sum(blocks, only_own):
        terms = blocks
        if not only_own:
            flat = blocks.reshape(n * cases, half)
            for f in range(6):
                moved = pltpu.roll(flat, half - 8 * (f + 1), 1).reshape(
                    sizes + (cases, half)
                )
                moved = jnp.roll(moved, 1 if f % 2 else -1, axis=f // 2)
                terms = terms + moved.reshape(n, cases, half)
        sums = [jnp.zeros((cases, half), jnp.float32) for _ in range(tiles_e)]
        for s in range(n):
            low = rigid * s
            moved = pltpu.roll(terms[s], low % half, 1) if low % half else terms[s]
            for q in range(low // half, (low + rigid - 1) // half + 1):
                at = lane + half * q
                sums[q] = jnp.where((at >= low) & (at < low + rigid), moved, sums[q])
        return jnp.concatenate(sums, axis=1)

    def own_inner(first, second):
        total = jnp.zeros((cases, half), jnp.float32)
        for f in range(6):
            cut = tile(own_tile(f))
            total = total + first[:, cut] * second[:, cut]
        return jnp.sum(total, axis=1, keepdims=True)

    def all_inner(first, second):
        total = jnp.zeros((cases, half), jnp.float32)
        for t in range(12):
            total = total + first[:, tile(t)] * second[:, tile(t)]
        return jnp.sum(total, axis=1, keepdims=True)

    split_chunk(0)
    split_chunk(1)
    for f in range(6):
        for i in range(2):
            set_all[f][i].wait_recv()
    residual = rvec[...]
    first_terms = dot_nt(residual, *split(bmat[0:8, :]))
    send_message(
        0, jnp.concatenate([first_terms, jnp.zeros((cases, half - 8), jnp.float32)], axis=1)
    )
    bhi[...], blo[...] = split(bmat[...])
    for c in range(2, 6):
        split_chunk(c)
    for f in range(6):
        set_all[f][2].wait_recv()
        for i in range(3):
            set_all[f][i].wait_send()
    chi[...], clo[...] = split(c7[...])
    gather_bytes(0).wait_recv()
    alpha = dot_nt(coarse_sum(received(0), True), chi[...], clo[...])
    active = act[...]
    z = residual - active * dot_nn(alpha, bhi[...], blo[...])

    face_copies = []
    lam = [jnp.zeros((cases, half), jnp.float32) for _ in range(6)]
    direction = image = alpha_image = energy = curvature = None
    for it in range(ITERS):
        last = it + 1 == ITERS
        p = it + 1
        parts = jnp.concatenate(split(z), axis=0)
        copies = [None] * 6
        ys = [None] * 6
        for f in (4, 5, 2, 3, 0, 1):
            yf = split_dot(parts, khi[f], klo[f], 0)
            yvec[it, f] = yf
            copy = remote(
                yvec.at[it, f], faces_in.at[it, f ^ 1], face_send.at[it, f],
                face_recv.at[it, f ^ 1], f,
            )
            copy.start()
            copies[f] = copy
            ys[f] = yf
        y = jnp.concatenate(ys, axis=1)
        scalars = [all_inner(z, y), own_inner(rvec, z)]
        if it:
            scalars.append(own_inner(z, image))
        if last:
            message = jnp.zeros((cases, half), jnp.float32)
        else:
            terms = dot_nt(y * active, bhi[...], blo[...])
            message = jnp.concatenate([terms, jnp.zeros_like(terms)], axis=1)
        for i, value in enumerate(scalars):
            message = jnp.where(lane == SCALARS + i, value, message)
        send_message(p, message)

        for f in range(6):
            copies[f].wait_recv()
        y = jnp.concatenate([ys[f] + faces_in[it, f] for f in range(6)], axis=1) * active
        gather_bytes(p).wait_recv()
        blocks = received(p)
        totals = jnp.sum(blocks, axis=0)
        along = totals[:, SCALARS : SCALARS + 1]
        energy_next = totals[:, SCALARS + 1 : SCALARS + 2]
        if it == 0:
            direction, image, curvature = z, y, along
        else:
            ratio = energy_next / energy
            across = totals[:, SCALARS + 2 : SCALARS + 3]
            direction = z + ratio * direction
            image = y + ratio * image
            curvature = along + 2.0 * ratio * across + ratio * ratio * curvature
        energy = energy_next
        step_size = energy / curvature
        rvec[...] = rvec[...] - step_size * image
        if not last:
            alpha_y = dot_nt(coarse_sum(blocks, False), chi[...], clo[...])
            alpha_image = alpha_y if it == 0 else alpha_y + ratio * alpha_image
            alpha = alpha - step_size * alpha_image
            z = rvec[...] - active * dot_nn(alpha, bhi[...], blo[...])
        for f in range(6):
            updated = lam[f] + step_size * direction[:, tile(own_tile(f))]
            lam[f] = jnp.where(contact[f] == 1, jnp.maximum(updated, 0.0), updated)
        face_copies.extend(copies)

    for f in range(6):
        lam_out[f] = lam[f]
        res_out[f] = rvec[:, tile(own_tile(f))]
    for copy in face_copies:
        copy.wait_send()
    for p in range(ITERS + 1):
        gather_bytes(p).wait_send()


def on_device(sizes, dual_matrix, modes, coarse_rows, loads, face_counts, contact):
    cases, faces, half = loads.shape[3:]
    local = dual_matrix.shape[-1]
    rigid = modes.shape[-2]
    full = 2 * half
    n = math.prod(sizes)
    width = -(-coarse_rows.shape[1] // half) * half
    hbm = pl.BlockSpec(memory_space=pl.ANY)
    vmem = pl.BlockSpec(memory_space=pltpu.VMEM)
    dma = pltpu.SemaphoreType.DMA
    f32 = jnp.float32
    out = jax.ShapeDtypeStruct((faces, cases, half), f32)
    lam, res = pl.pallas_call(
        functools.partial(kernel, sizes),
        out_shape=(out, out),
        in_specs=[
            hbm,
            hbm,
            hbm,
            hbm,
            pl.BlockSpec(memory_space=pltpu.SMEM),
            hbm,
        ],
        out_specs=(vmem, vmem),
        scratch_shapes=[
            pltpu.VMEM((faces, local, full), f32),
            pltpu.VMEM((faces, local, full), jnp.bfloat16),
            pltpu.VMEM((faces, local, full), jnp.bfloat16),
            pltpu.VMEM((64, local), f32),
            pltpu.VMEM((64, width), f32),
            pltpu.VMEM((cases, local), f32),
            pltpu.VMEM((cases, local), f32),
            pltpu.VMEM((ITERS, faces, cases, full), f32),
            pltpu.VMEM((ITERS, faces, cases, full), f32),
            pltpu.VMEM((ITERS + 1, n, cases // 2, half), f32),
            pltpu.VMEM((rigid, 1, local), f32),
            pltpu.VMEM(coarse_rows.shape, f32),
            pltpu.VMEM((faces, cases, half), f32),
            pltpu.VMEM((faces, 1, half), jnp.int32),
            pltpu.VMEM((64, local), jnp.bfloat16),
            pltpu.VMEM((64, local), jnp.bfloat16),
            pltpu.VMEM((64, width), jnp.bfloat16),
            pltpu.VMEM((64, width), jnp.bfloat16),
            dma((faces,)),
            dma((4,)),
            dma((faces, 3)),
            dma((faces, 3)),
            dma((ITERS, faces)),
            dma((ITERS, faces)),
            dma((ITERS + 1,)),
            dma((ITERS + 1,)),
        ],
        compiler_params=pltpu.CompilerParams(
            collective_id=0, has_side_effects=True, vmem_limit_bytes=64 * 1024 * 1024
        ),
    )(
        dual_matrix.reshape(local, local),
        modes.reshape(rigid, 1, local),
        coarse_rows,
        loads.reshape(cases, faces, half).transpose(1, 0, 2),
        face_counts.transpose(0, 3, 1, 2),
        contact.reshape(faces, 1, half),
    )
    return (
        lam.transpose(1, 0, 2).reshape(loads.shape),
        res.transpose(1, 0, 2).reshape(loads.shape),
    )


def solution(mesh):
    sizes = tuple(mesh.shape[name] for name in NAMES)
    return jax.shard_map(
        functools.partial(on_device, sizes),
        mesh=mesh,
        in_specs=(
            P("gx", "gy", "gz", None, None),
            P("gx", "gy", "gz", None, None),
            P(("gx", "gy", "gz"), None),
            P("gx", "gy", "gz", None, None, None),
            P(),
            P("gx", "gy", "gz", None, None),
        ),
        out_specs=(P("gx", "gy", "gz", None, None, None), P("gx", "gy", "gz", None, None, None)),
        check_vma=False,
    )
```

```python
import functools
import math

import jax
import jax.numpy as jnp
from jax import lax
from jax.experimental import pallas as pl
from jax.experimental.pallas import tpu as pltpu
from jax.sharding import PartitionSpec as P

ITERS = 4
NAMES = ("gx", "gy", "gz")
SCALARS = 56


def split(x):
    hi = x.astype(jnp.bfloat16)
    return hi, (x - hi.astype(jnp.float32)).astype(jnp.bfloat16)


def split_dot(parts, hi, lo, contract):
    dims = (((1,), (contract,)), ((), ()))
    both = lax.dot_general(parts, hi, dims, preferred_element_type=jnp.float32)
    both = both + lax.dot_general(parts, lo, dims, preferred_element_type=jnp.float32)
    rows = parts.shape[0] // 2
    return both[0:rows] + both[rows:]


def dot_nt(a, hi, lo):
    return split_dot(jnp.concatenate(split(a), axis=0), hi, lo, 1)


def dot_nn(a, hi, lo):
    return split_dot(jnp.concatenate(split(a), axis=0), hi, lo, 0)


def kernel(
    sizes,
    k_hbm,
    modes_in,
    crows_in,
    loads_in,
    counts,
    contact_in,
    lam_out,
    res_out,
    kbuf,
    khi,
    klo,
    bmat,
    c7,
    act,
    rvec,
    yvec,
    faces_in,
    gath,
    modes,
    crows,
    loads,
    contact,
    bhi,
    blo,
    chi,
    clo,
    k_sem,
    in_sem,
    set_send,
    set_recv,
    face_send,
    face_recv,
    gath_send,
    gath_recv,
):
    cases = loads.shape[1]
    half = loads.shape[2]
    full = 2 * half
    local = bmat.shape[1]
    rigid = modes_in.shape[0]
    n = math.prod(sizes)
    pos = [lax.axis_index(name) for name in NAMES]
    me = (pos[0] * sizes[1] + pos[1]) * sizes[2] + pos[2]

    def neighbour(f):
        a = f // 2
        step = 1 if f % 2 else sizes[a] - 1
        where = list(pos)
        where[a] = lax.rem(pos[a] + step, sizes[a])
        return tuple(where)

    nbrs = [neighbour(f) for f in range(6)]

    def own_tile(f):
        return 2 * f + (1 - f % 2)

    def tile(f_tile):
        return slice(f_tile * half, (f_tile + 1) * half)

    def k_copy(c):
        return pltpu.make_async_copy(
            k_hbm.at[:, pl.ds(c * full, full)], kbuf.at[c], k_sem.at[c]
        )

    small = [
        pltpu.make_async_copy(src, dst, in_sem.at[i])
        for i, (src, dst) in enumerate(
            ((loads_in, loads), (modes_in, modes), (crows_in, crows), (contact_in, contact))
        )
    ]
    for copy in small:
        copy.start()
    for c in range(6):
        k_copy(c).start()

    bmat[...] = jnp.zeros_like(bmat)
    c7[...] = jnp.zeros_like(c7)
    barrier = pltpu.get_barrier_semaphore()

    def greet(k, carry):
        pl.semaphore_signal(
            barrier,
            inc=1,
            device_id=lax.rem(me + k, n),
            device_id_type=pl.DeviceIdType.LOGICAL,
        )
        return carry

    lax.fori_loop(1, n, greet, 0)
    for copy in small:
        copy.wait()
    for m in range(rigid):
        bmat[m : m + 1, :] = modes[m]
    c7[0:rigid, 0 : crows.shape[1]] = crows[...]

    lane = lax.broadcasted_iota(jnp.int32, (cases, half), 1)
    for f in range(6):
        a = f // 2
        where = list(pos) if f % 2 else list(nbrs[f])
        count = counts[where[0], a, where[1], where[2]]
        mask = (lane < count).astype(jnp.float32)
        act[:, tile(2 * f)] = mask
        act[:, tile(2 * f + 1)] = mask
        rvec[:, tile(own_tile(f))] = loads[f] * mask

    pl.semaphore_wait(barrier, n - 1)

    def remote(src, dst, send, recv, f):
        return pltpu.make_async_remote_copy(
            src_ref=src,
            dst_ref=dst,
            send_sem=send,
            recv_sem=recv,
            device_id=nbrs[f],
            device_id_type=pl.DeviceIdType.MESH,
        )

    def set_copies(f):
        opp = f ^ 1
        h = 1 - f % 2
        rows = pl.ds(8 * (opp + 1), 8)
        return [
            remote(
                rvec.at[:, pl.ds((2 * f + h) * half, half)],
                rvec.at[:, pl.ds((2 * opp + h) * half, half)],
                set_send.at[f, 0],
                set_recv.at[opp, 0],
                f,
            ),
            remote(
                bmat.at[pl.ds(0, 8), pl.ds(f * full, full)],
                bmat.at[rows, pl.ds(opp * full, full)],
                set_send.at[f, 1],
                set_recv.at[opp, 1],
                f,
            ),
            remote(c7.at[pl.ds(0, 8)], c7.at[rows], set_send.at[f, 2], set_recv.at[opp, 2], f),
        ]

    set_all = [set_copies(f) for f in range(6)]
    for i in range(3):
        for f in range(6):
            set_all[f][i].start()

    def split_chunk(c):
        k_copy(c).wait()
        step = 256

        def body(i, carry):
            rows = pl.ds(pl.multiple_of(i * step, step), step)
            x = kbuf[c, rows, :]
            khi[c, rows, :], klo[c, rows, :] = split(x)
            return carry

        lax.fori_loop(0, local // step, body, 0)

    def send_message(p, message):
        rolled = pltpu.roll(message, half // 2, 1)
        packed = jnp.where(
            lane[0 : cases // 2] < half // 2, message[0 : cases // 2], rolled[cases // 2 :]
        )
        gath[p, me] = packed

        def body(k, carry):
            pltpu.make_async_remote_copy(
                src_ref=gath.at[p, me],
                dst_ref=gath.at[p, me],
                send_sem=gath_send.at[p],
                recv_sem=gath_recv.at[p],
                device_id=lax.rem(me + k, n),
                device_id_type=pl.DeviceIdType.LOGICAL,
            ).start()
            return carry

        lax.fori_loop(1, n, body, 0)

    def gather_bytes(p):
        block = gath.at[p, pl.ds(0, n - 1)]
        return pltpu.make_async_remote_copy(
            src_ref=block,
            dst_ref=block,
            send_sem=gath_send.at[p],
            recv_sem=gath_recv.at[p],
            device_id=lax.rem(me + 1, n),
            device_id_type=pl.DeviceIdType.LOGICAL,
        )

    def received(p):
        packed = gath[p]
        other = pltpu.roll(packed.reshape(n * cases // 2, half), half // 2, 1).reshape(
            packed.shape
        )
        return jnp.concatenate([packed, other], axis=1)

    tiles_e = c7.shape[1] // half

    def coarse_sum(blocks, only_own):
        terms = blocks
        if not only_own:
            flat = blocks.reshape(n * cases, half)
            for f in range(6):
                moved = pltpu.roll(flat, half - 8 * (f + 1), 1).reshape(
                    sizes + (cases, half)
                )
                moved = jnp.roll(moved, 1 if f % 2 else -1, axis=f // 2)
                terms = terms + moved.reshape(n, cases, half)
        sums = [jnp.zeros((cases, half), jnp.float32) for _ in range(tiles_e)]
        for s in range(n):
            low = rigid * s
            moved = pltpu.roll(terms[s], low % half, 1) if low % half else terms[s]
            for q in range(low // half, (low + rigid - 1) // half + 1):
                at = lane + half * q
                sums[q] = jnp.where((at >= low) & (at < low + rigid), moved, sums[q])
        return jnp.concatenate(sums, axis=1)

    def own_inner(first, second):
        total = jnp.zeros((cases, half), jnp.float32)
        for f in range(6):
            cut = tile(own_tile(f))
            total = total + first[:, cut] * second[:, cut]
        return jnp.sum(total, axis=1, keepdims=True)

    def all_inner(first, second):
        total = jnp.zeros((cases, half), jnp.float32)
        for t in range(12):
            total = total + first[:, tile(t)] * second[:, tile(t)]
        return jnp.sum(total, axis=1, keepdims=True)

    split_chunk(0)
    split_chunk(1)
    for f in range(6):
        for i in range(2):
            set_all[f][i].wait_recv()
    residual = rvec[...]
    first_terms = dot_nt(residual, *split(bmat[0:8, :]))
    send_message(
        0, jnp.concatenate([first_terms, jnp.zeros((cases, half - 8), jnp.float32)], axis=1)
    )
    bhi[...], blo[...] = split(bmat[...])
    for c in range(2, 6):
        split_chunk(c)
    for f in range(6):
        set_all[f][2].wait_recv()
        for i in range(3):
            set_all[f][i].wait_send()
    chi[...], clo[...] = split(c7[...])
    gather_bytes(0).wait_recv()
    alpha = dot_nt(coarse_sum(received(0), True), chi[...], clo[...])
    active = act[...]
    z = residual - active * dot_nn(alpha, bhi[...], blo[...])

    face_copies = []
    lam = [jnp.zeros((cases, half), jnp.float32) for _ in range(6)]
    direction = image = alpha_image = energy = curvature = None
    for it in range(ITERS):
        last = it + 1 == ITERS
        p = it + 1
        parts = jnp.concatenate(split(z), axis=0)
        copies = [None] * 6
        ys = [None] * 6
        for f in (4, 5, 2, 3, 0, 1):
            yf = split_dot(parts, khi[f], klo[f], 0)
            yvec[it, f] = yf
            copy = remote(
                yvec.at[it, f], faces_in.at[it, f ^ 1], face_send.at[it, f],
                face_recv.at[it, f ^ 1], f,
            )
            copies[f] = copy
            ys[f] = yf
        y = jnp.concatenate(ys, axis=1)
        scalars = [all_inner(z, y), own_inner(rvec, z)]
        if it:
            scalars.append(own_inner(z, image))
        if last:
            message = jnp.zeros((cases, half), jnp.float32)
        else:
            terms = dot_nt(y * active, bhi[...], blo[...])
            message = jnp.concatenate([terms, jnp.zeros_like(terms)], axis=1)
        for i, value in enumerate(scalars):
            message = jnp.where(lane == SCALARS + i, value, message)
        send_message(p, message)
        for f in (4, 5, 2, 3, 0, 1):
            copies[f].start()

        for f in range(6):
            copies[f].wait_recv()
        y = jnp.concatenate([ys[f] + faces_in[it, f] for f in range(6)], axis=1) * active
        gather_bytes(p).wait_recv()
        blocks = received(p)
        totals = jnp.sum(blocks, axis=0)
        along = totals[:, SCALARS : SCALARS + 1]
        energy_next = totals[:, SCALARS + 1 : SCALARS + 2]
        if it == 0:
            direction, image, curvature = z, y, along
        else:
            ratio = energy_next / energy
            across = totals[:, SCALARS + 2 : SCALARS + 3]
            direction = z + ratio * direction
            image = y + ratio * image
            curvature = along + 2.0 * ratio * across + ratio * ratio * curvature
        energy = energy_next
        step_size = energy / curvature
        rvec[...] = rvec[...] - step_size * image
        if not last:
            alpha_y = dot_nt(coarse_sum(blocks, False), chi[...], clo[...])
            alpha_image = alpha_y if it == 0 else alpha_y + ratio * alpha_image
            alpha = alpha - step_size * alpha_image
            z = rvec[...] - active * dot_nn(alpha, bhi[...], blo[...])
        for f in range(6):
            updated = lam[f] + step_size * direction[:, tile(own_tile(f))]
            lam[f] = jnp.where(contact[f] == 1, jnp.maximum(updated, 0.0), updated)
        face_copies.extend(copies)

    for f in range(6):
        lam_out[f] = lam[f]
        res_out[f] = rvec[:, tile(own_tile(f))]
    for copy in face_copies:
        copy.wait_send()
    for p in range(ITERS + 1):
        gather_bytes(p).wait_send()


def on_device(sizes, dual_matrix, modes, coarse_rows, loads, face_counts, contact):
    cases, faces, half = loads.shape[3:]
    local = dual_matrix.shape[-1]
    rigid = modes.shape[-2]
    full = 2 * half
    n = math.prod(sizes)
    width = -(-coarse_rows.shape[1] // half) * half
    hbm = pl.BlockSpec(memory_space=pl.ANY)
    vmem = pl.BlockSpec(memory_space=pltpu.VMEM)
    dma = pltpu.SemaphoreType.DMA
    f32 = jnp.float32
    out = jax.ShapeDtypeStruct((faces, cases, half), f32)
    lam, res = pl.pallas_call(
        functools.partial(kernel, sizes),
        out_shape=(out, out),
        in_specs=[
            hbm,
            hbm,
            hbm,
            hbm,
            pl.BlockSpec(memory_space=pltpu.SMEM),
            hbm,
        ],
        out_specs=(vmem, vmem),
        scratch_shapes=[
            pltpu.VMEM((faces, local, full), f32),
            pltpu.VMEM((faces, local, full), jnp.bfloat16),
            pltpu.VMEM((faces, local, full), jnp.bfloat16),
            pltpu.VMEM((64, local), f32),
            pltpu.VMEM((64, width), f32),
            pltpu.VMEM((cases, local), f32),
            pltpu.VMEM((cases, local), f32),
            pltpu.VMEM((ITERS, faces, cases, full), f32),
            pltpu.VMEM((ITERS, faces, cases, full), f32),
            pltpu.VMEM((ITERS + 1, n, cases // 2, half), f32),
            pltpu.VMEM((rigid, 1, local), f32),
            pltpu.VMEM(coarse_rows.shape, f32),
            pltpu.VMEM((faces, cases, half), f32),
            pltpu.VMEM((faces, 1, half), jnp.int32),
            pltpu.VMEM((64, local), jnp.bfloat16),
            pltpu.VMEM((64, local), jnp.bfloat16),
            pltpu.VMEM((64, width), jnp.bfloat16),
            pltpu.VMEM((64, width), jnp.bfloat16),
            dma((faces,)),
            dma((4,)),
            dma((faces, 3)),
            dma((faces, 3)),
            dma((ITERS, faces)),
            dma((ITERS, faces)),
            dma((ITERS + 1,)),
            dma((ITERS + 1,)),
        ],
        compiler_params=pltpu.CompilerParams(
            collective_id=0, has_side_effects=True, vmem_limit_bytes=64 * 1024 * 1024
        ),
    )(
        dual_matrix.reshape(local, local),
        modes.reshape(rigid, 1, local),
        coarse_rows,
        loads.reshape(cases, faces, half).transpose(1, 0, 2),
        face_counts.transpose(0, 3, 1, 2),
        contact.reshape(faces, 1, half),
    )
    return (
        lam.transpose(1, 0, 2).reshape(loads.shape),
        res.transpose(1, 0, 2).reshape(loads.shape),
    )


def solution(mesh):
    sizes = tuple(mesh.shape[name] for name in NAMES)
    return jax.shard_map(
        functools.partial(on_device, sizes),
        mesh=mesh,
        in_specs=(
            P("gx", "gy", "gz", None, None),
            P("gx", "gy", "gz", None, None),
            P(("gx", "gy", "gz"), None),
            P("gx", "gy", "gz", None, None, None),
            P(),
            P("gx", "gy", "gz", None, None),
        ),
        out_specs=(P("gx", "gy", "gz", None, None, None), P("gx", "gy", "gz", None, None, None)),
        check_vma=False,
    )
```
